128 devices in a mesh: row: 32 (over y, x, core), col: 4 (over z).
Axes of the slice: x: 4, y: 4, z: 4, core: 2. Of those that a mesh axis runs over, the one named last changes fastest.
Arguments:
- acts: bfloat16 [122880, 6144], P(('row', 'col')), may hold values from -6 to 6
- out_grads: bfloat16 [122880, 6144], P(('row', 'col')), may hold values from -6 to 6
- test_matrix: bfloat16 [6144, 64], replicated, may hold values from -6 to 6
- weight: bfloat16 [6144, 6144], P('row', 'col'), may hold values from -6 to 6
Outputs:
- frozen: float32 [6144, 6144], P('row', 'col')
- adapter_left_factor: float32 [6144, 64], P('row')
- adapter_right_factor: float32 [64, 6144], P(None, 'col')
The draws below stay inside these ranges and needn't reach their ends.
All inputs are finite; a program needn't handle non-finite values.
Results may differ from the reference program's by a relative error of at most 0.0035.
Values may be sent and summed in bfloat16 or wider, within the bound.
No kernel may reach another device: no remote copies, remote signals or barrier semaphores. Data moves between devices by JAX's collectives and lax.ppermute only.
A program may use at most 128 MiB of HBM per device.

```python
import math
import jax
import jax.numpy as jnp
from jax import lax

OUTPUT_FEATURES = 6144
INPUT_FEATURES = 6144
RANK = 64
TOKENS = 122880


def shared_factor(key, top):
    latent_key = jax.random.fold_in(key, 100)
    strength_key = jax.random.fold_in(key, 101)
    latent = jax.random.normal(latent_key, (TOKENS, RANK), jnp.float32)
    strengths = jnp.exp(jax.random.uniform(strength_key, (RANK,), jnp.float32, 0.0, math.log(top)))
    return (latent, strengths)


def noise_normal(key, width):
    return jax.random.normal(key, (TOKENS, width), jnp.float32)


def mixed_rows(latent, weights, directions, noise, scale):
    low_part = jnp.dot(latent * weights[None, :], directions, precision=lax.Precision.HIGHEST, preferred_element_type=jnp.float32)
    total = math.sqrt(0.5) * low_part / scale + math.sqrt(0.5) * noise
    return jnp.clip(total, -6.0, 6.0)


def draw_acts(key, part):
    latent, strengths = shared_factor(key, 4.0)
    key = jax.random.fold_in(key, 1)
    directions = jax.random.normal(jax.random.fold_in(key, 2), (RANK, INPUT_FEATURES), jnp.float32)
    noise = noise_normal(jax.random.fold_in(key, 3), INPUT_FEATURES)
    unit = jnp.ones((RANK,), jnp.float32)
    return mixed_rows(latent, unit, directions, noise, math.sqrt(RANK)).astype(jnp.bfloat16)


def draw_out_grads(key, part):
    latent, strengths = shared_factor(key, 4.0)
    scale = 2.5 * math.sqrt(RANK)
    key = jax.random.fold_in(key, 5)
    directions = jax.random.normal(jax.random.fold_in(key, 6), (RANK, OUTPUT_FEATURES), jnp.float32)
    noise = noise_normal(jax.random.fold_in(key, 7), OUTPUT_FEATURES)
    return mixed_rows(latent, strengths, directions, noise, scale).astype(jnp.bfloat16)


def levels(key, shape, split, low, high):
    loudness = 1.0
    for position, blocks in split:
        draws = jax.random.uniform(jax.random.fold_in(jax.random.fold_in(key, 6), position), (blocks,), jnp.float32, low / len(split), high / len(split))
        loudness = loudness * jnp.repeat(jnp.exp(draws), shape[position] // blocks).reshape((-1,) + (1,) * (len(shape) - 1 - position))
    return loudness


def scatter_about(stream_key, extent, deviation, limit, split=(), kind=jnp.bfloat16):
    result = deviation * jax.random.normal(stream_key, extent, jnp.float32)
    if split:
        result = result * levels(stream_key, extent, split, -0.22, 0.18)
    return jnp.clip(result, -limit, limit).astype(kind)


def setup_inputs(seed: int = 0) -> dict:
    arg_keys = jax.random.split(jax.random.key(seed), 5)
    return {
        "acts": draw_acts(jax.random.fold_in(arg_keys[4], 71), 0),
        "out_grads": draw_out_grads(jax.random.fold_in(arg_keys[4], 71), 0),
        "test_matrix": scatter_about(arg_keys[2], (INPUT_FEATURES, RANK), 1.0, 6.0),
        "weight": scatter_about(arg_keys[3], (OUTPUT_FEATURES, INPUT_FEATURES), 1.0, 6.0, ((0, 32), (1, 4))),
    }


def cholqr(block):
    gram = jnp.dot(block.T.astype(jnp.float32), block.astype(jnp.float32), precision=lax.Precision.HIGHEST, preferred_element_type=jnp.float32)
    lower = jnp.linalg.cholesky(gram)
    return jax.scipy.linalg.solve_triangular(lower, block.T, lower=True).T

def reference(acts, out_grads, test_matrix, weight):
    probe = jnp.dot(acts.astype(jnp.float32), test_matrix.astype(jnp.float32), preferred_element_type=jnp.float32).astype(jnp.bfloat16)
    sketch = jnp.dot(out_grads.T.astype(jnp.float32), probe.astype(jnp.float32), preferred_element_type=jnp.float32)
    basis_low = cholqr(sketch).astype(jnp.bfloat16)
    back = jnp.dot(out_grads.astype(jnp.float32), basis_low.astype(jnp.float32), preferred_element_type=jnp.float32).astype(jnp.bfloat16)
    cosketch = jnp.dot(acts.T.astype(jnp.float32), back.astype(jnp.float32), preferred_element_type=jnp.float32)
    cobasis_low = cholqr(cosketch).astype(jnp.bfloat16)
    forth = jnp.dot(acts.astype(jnp.float32), cobasis_low.astype(jnp.float32), preferred_element_type=jnp.float32).astype(jnp.bfloat16)
    power = jnp.dot(out_grads.T.astype(jnp.float32), forth.astype(jnp.float32), preferred_element_type=jnp.float32)
    left_factor = cholqr(power)
    left_low = left_factor.astype(jnp.bfloat16)
    again = jnp.dot(out_grads.astype(jnp.float32), left_low.astype(jnp.float32), preferred_element_type=jnp.float32).astype(jnp.bfloat16)
    project = jnp.dot(acts.T.astype(jnp.float32), again.astype(jnp.float32), preferred_element_type=jnp.float32)
    right_factor = cholqr(project)
    adapter_left_factor = left_factor * math.sqrt(OUTPUT_FEATURES)
    adapter_right_factor = right_factor.T * math.sqrt(INPUT_FEATURES)
    product_matrix = jnp.dot(adapter_left_factor.astype(jnp.float32), adapter_right_factor.astype(jnp.float32), precision=lax.Precision.HIGHEST, preferred_element_type=jnp.float32)
    frozen = weight.astype(jnp.float32) - product_matrix / math.sqrt(RANK)
    return (frozen, adapter_left_factor, adapter_right_factor)
```

```python
import math

import jax
import jax.numpy as jnp
from jax import lax
from jax.sharding import Mesh, PartitionSpec as P

CHIPS = ("y", "x", "z")
HIGHEST = lax.Precision.HIGHEST


def to_parts(wide):
    rank, n = wide.shape
    parts = wide.reshape(2, 4, 8, 16, n // 16).transpose(0, 1, 3, 2, 4)
    return parts.reshape(2, 64, 8, n // 16)


def from_parts(parts):
    _, _, rows, lanes = parts.shape
    wide = parts.reshape(2, 4, 16, rows, lanes).transpose(0, 1, 3, 2, 4)
    return wide.reshape(8 * rows, 16 * lanes)


def swap_cores(value):
    return lax.ppermute(value, "core", [(0, 1), (1, 0)])


def total(wide):
    parts = to_parts(wide)
    core = lax.axis_index("core")
    own = lax.dynamic_index_in_dim(parts, core, 0, keepdims=False)
    other = lax.dynamic_index_in_dim(parts, 1 - core, 0, keepdims=False)
    got = swap_cores(other.astype(jnp.bfloat16))
    pair = (own + got.astype(jnp.float32)).astype(jnp.bfloat16)
    terms = lax.all_to_all(pair, CHIPS, 0, 0, tiled=True)
    mine = jnp.sum(terms.astype(jnp.float32), axis=0)
    copies = jnp.broadcast_to(mine[None], terms.shape)
    half = lax.all_to_all(copies, CHIPS, 0, 0, tiled=True)
    return from_parts(lax.all_gather(half, "core", axis=0, tiled=False))


def inverse_factor(wide):
    wide = wide.astype(jnp.float32)
    gram = lax.dot_general(
        wide, wide, (((1,), (1,)), ((), ())), precision=HIGHEST,
        preferred_element_type=jnp.float32,
    )
    lower = jnp.linalg.cholesky(gram)
    return jax.scipy.linalg.solve_triangular(lower, jnp.eye(64, dtype=jnp.float32), lower=True)


def product(left, right, contract):
    return lax.dot_general(
        left, right, ((contract[:1], contract[1:]), ((), ())),
        preferred_element_type=jnp.float32,
    )


def exact(left, right):
    return jnp.dot(left, right, precision=HIGHEST, preferred_element_type=jnp.float32)


def step(tokens, wide, other):
    basis = exact(inverse_factor(wide), wide).astype(jnp.bfloat16)
    applied = product(basis, tokens, (1, 1)).astype(jnp.bfloat16)
    return product(applied, other, (1, 0))


def local(acts, out_grads, test_matrix, weight):
    rows, cols = weight.shape
    n = acts.shape[1]
    row = (lax.axis_index("y") * 4 + lax.axis_index("x")) * 2 + lax.axis_index("core")
    col = lax.axis_index("z")
    probe = product(test_matrix, acts, (0, 1)).astype(jnp.bfloat16)
    sketch = total(product(probe, out_grads, (1, 0)))
    cosketch = total(step(out_grads, sketch, acts))
    power = total(step(acts, cosketch, out_grads))
    project = total(step(out_grads, power, acts))
    left = exact(
        inverse_factor(power), lax.dynamic_slice_in_dim(power, row * rows, rows, 1)
    )
    right = exact(
        inverse_factor(project), lax.dynamic_slice_in_dim(project, col * cols, cols, 1)
    )
    left = left.T * math.sqrt(n)
    right = right * math.sqrt(n)
    frozen = weight.astype(jnp.float32) - exact(left, right) / math.sqrt(64)
    return (frozen, left, right)


def solution(mesh):
    mesh = Mesh(mesh.devices.reshape(4, 4, 2, 4), ("y", "x", "core", "z"))
    row = ("y", "x", "core")
    tokens = P((*row, "z"), None)
    return jax.shard_map(
        local, mesh=mesh, in_specs=(tokens, tokens, P(), P(row, "z")),
        out_specs=(P(row, "z"), P(row, None), P(None, "z")), check_vma=False,
    )
```

```python
import math

import jax
import jax.numpy as jnp
from jax import lax
from jax.experimental import pallas as pl
from jax.experimental.pallas import tpu as pltpu
from jax.sharding import Mesh, PartitionSpec as P

CHIPS = ("y", "x", "z")
F32 = jnp.float32
BF16 = jnp.bfloat16
RANK = 64
VMEM = pl.BlockSpec(memory_space=pltpu.VMEM)
ANY = pl.BlockSpec(memory_space=pl.ANY)
PARAMS = pltpu.CompilerParams(vmem_limit_bytes=56 * 2**20)
GROUPS = 4
LANES = 16


def dot(left, right, contract):
    dims = (((contract[0],), (contract[1],)), ((), ()))
    return lax.dot_general(left, right, dims, preferred_element_type=F32)


def split(value):
    high = value.astype(BF16)
    return high, (value - high.astype(F32)).astype(BF16)


def exact(left, right):
    left_high, left_low = split(left)
    right_high, right_low = split(right)
    return dot(
        jnp.concatenate([left_high, left_high, left_low], 1),
        jnp.concatenate([right_high, right_low, right_high], 0),
        (1, 0),
    )


def inverse_factor(gram):
    shape = (RANK, RANK)
    eye = lax.broadcasted_iota(jnp.int32, shape, 0) == lax.broadcasted_iota(jnp.int32, shape, 1)
    both = jnp.concatenate([gram, eye.astype(F32)], 1)
    work = [both[8 * i : 8 * i + 8] for i in range(8)]
    tile = (8, 2 * RANK)
    sub = lax.broadcasted_iota(jnp.int32, tile, 0)
    done = []
    for p in range(8):
        cols = {
            i: [jnp.broadcast_to(work[i][:, k : k + 1], tile) for k in range(8 * p, 8 * p + 8)]
            for i in range(p, 8)
        }
        pivots = jnp.zeros(tile, F32)
        for j in range(8):
            pivot = jnp.broadcast_to(cols[p][j][j : j + 1], tile)
            inverse = 1.0 / pivot
            pivots = jnp.where(sub == j, pivot, pivots)
            row = jnp.broadcast_to(work[p][j : j + 1], tile)
            ahead = {q: jnp.broadcast_to(cols[p][q][j : j + 1], tile) for q in range(j + 1, 8)}
            for i in range(p, 8):
                scale = cols[i][j] * inverse
                if i == p:
                    scale = jnp.where(sub > j, scale, 0.0)
                work[i] = work[i] - scale * row
                for q in range(j + 1, 8):
                    cols[i][q] = cols[i][q] - scale * ahead[q]
        done.append(work[p] * lax.rsqrt(pivots))
    return jnp.concatenate(done, 0)[:, RANK:]


def wide_block(first, own_ref, other_ref, lane):
    own = [own_ref[g * LANES + lane] for g in range(GROUPS)]
    other = [other_ref[g * LANES + lane] for g in range(GROUPS)]
    low = [jnp.where(first, a, b) for a, b in zip(own, other)]
    high = [jnp.where(first, b, a) for a, b in zip(own, other)]
    return jnp.concatenate(low + high, 0)


def gram_of(first, own_ref, other_ref, split_ref=None):
    width = own_ref.shape[2]
    gram = jnp.zeros((2 * RANK, 2 * RANK), F32)
    for lane in range(LANES):
        terms = jnp.concatenate(split(wide_block(first, own_ref, other_ref, lane)), 0)
        if split_ref is not None:
            split_ref[:, lane * width : (lane + 1) * width] = terms
        gram = gram + dot(terms, terms, (1, 1))
    cross = gram[:RANK, RANK:] + gram[RANK:, :RANK]
    return gram[:RANK, :RANK] + (gram[RANK:, RANK:] + cross)


def store_parts(first, part, index, keep_ref, send_ref):
    width = keep_ref.shape[2]
    for h in range(2):
        for g in range(GROUPS):
            low = part[8 * g : 8 * g + 8, h * width : (h + 1) * width]
            high = part[32 + 8 * g : 40 + 8 * g, h * width : (h + 1) * width]
            at = g * LANES + 2 * index + h
            keep_ref[at] = jnp.where(first, low, high)
            send_ref[at] = jnp.where(first, high, low).astype(BF16)


def chunks(total, size):
    return [(s, min(size, total - s)) for s in range(0, total, size)]


def row_copies(ref, held, sems):
    return [
        pltpu.make_async_copy(ref.at[pl.ds(s, n), :], held.at[pl.ds(s, n), :], sems.at[i])
        for i, (s, n) in enumerate(chunks(ref.shape[0], 256))
    ]


def col_copies(ref, held, sems):
    return [
        pltpu.make_async_copy(ref.at[:, pl.ds(s, n)], held.at[:, pl.ds(s, n)], sems.at[i])
        for i, (s, n) in enumerate(chunks(ref.shape[1], ref.shape[1] // 8))
    ]


def first_kernel(test_ref, a_ref, b_ref, keep_ref, send_ref, a_held, b_held, a_sems, b_sems):
    first = lax.axis_index("core") == 0
    a_copies = row_copies(a_ref, a_held, a_sems)
    b_copies = col_copies(b_ref, b_held, b_sems)
    for copy in a_copies + b_copies:
        copy.start()
    test = test_ref[...]
    applied = []
    for copy, (s, n) in zip(a_copies, chunks(a_ref.shape[0], 256)):
        copy.wait()
        applied.append(dot(a_held[s : s + n, :], test, (1, 0)).astype(BF16))
    applied = jnp.concatenate(applied, 0)
    for i, (copy, (s, n)) in enumerate(zip(b_copies, chunks(b_ref.shape[1], b_ref.shape[1] // 8))):
        copy.wait()
        store_parts(first, dot(applied, b_held[:, s : s + n], (0, 0)), i, keep_ref, send_ref)


def next_kernel(
    own_ref, other_ref, a_ref, b_ref, keep_ref, send_ref, *rest
):
    left_ref = rest[0] if len(rest) == 7 else None
    a_held, b_held, split_held, left_held, a_sems, b_sems = rest[-6:]
    core = lax.axis_index("core")
    first = core == 0
    a_copies = row_copies(a_ref, a_held, a_sems)
    b_copies = col_copies(b_ref, b_held, b_sems)
    for copy in a_copies + b_copies:
        copy.start()
    gram = gram_of(first, own_ref, other_ref, split_held)
    for copy in a_copies:
        copy.wait()
    inverse = inverse_factor(gram)
    raw = dot(split_held[...], a_held[...], (1, 1))
    applied = exact(inverse, raw[:RANK] + raw[RANK:]).astype(BF16)
    for i, (copy, (s, n)) in enumerate(zip(b_copies, chunks(b_ref.shape[1], b_ref.shape[1] // 8))):
        copy.wait()
        store_parts(first, dot(applied, b_held[:, s : s + n], (1, 0)), i, keep_ref, send_ref)
    if left_ref is not None:
        lane = lax.axis_index("y") * 4 + lax.axis_index("x")
        rows = left_ref.shape[0]
        left = exact(inverse, wide_block(first, own_ref, other_ref, lane)).T
        left_held[...] = left * math.sqrt(a_ref.shape[1])
        left_ref[...] = left_held[pl.ds(pl.multiple_of(core * rows, rows), rows), :]


def last_kernel(own_ref, other_ref, left_ref, weight_ref, frozen_ref, right_ref):
    first = lax.axis_index("core") == 0
    inverse = inverse_factor(gram_of(first, own_ref, other_ref))
    width = own_ref.shape[2]
    left = left_ref[...]
    for q in range(4):
        block = wide_block(first, own_ref, other_ref, lax.axis_index("z") * 4 + q)
        right = exact(inverse, block) * math.sqrt(LANES * width)
        at = slice(q * width, (q + 1) * width)
        right_ref[:, at] = right
        frozen_ref[:, at] = weight_ref[:, at].astype(F32) - exact(left, right) / math.sqrt(RANK)


def total(keep, send):
    got = lax.ppermute(send, "core", [(0, 1), (1, 0)])
    pair = (keep + got.astype(F32)).astype(BF16)
    terms = lax.all_to_all(pair, CHIPS, 0, 0, tiled=True)
    mine = jnp.sum(terms.astype(F32), axis=0)
    copies = jnp.broadcast_to(mine[None], terms.shape)
    own = lax.all_to_all(copies, CHIPS, 0, 0, tiled=True)
    return own, lax.ppermute(own, "core", [(0, 1), (1, 0)])


def local(acts, out_grads, test_matrix, weight):
    tokens, n = acts.shape
    rows, cols = weight.shape
    parts = (LANES * GROUPS, 8, n // LANES)
    partial = (jax.ShapeDtypeStruct(parts, F32), jax.ShapeDtypeStruct(parts, BF16))
    held = [pltpu.VMEM((tokens, n), BF16)] * 2
    sems = [pltpu.SemaphoreType.DMA((len(chunks(tokens, 256)),)), pltpu.SemaphoreType.DMA((8,))]
    sketch = total(*pl.pallas_call(
        first_kernel, out_shape=partial, in_specs=[VMEM, ANY, ANY], out_specs=(VMEM, VMEM),
        scratch_shapes=[*held, *sems], compiler_params=PARAMS, name="first",
    )(test_matrix, acts, out_grads))

    def step(name, wide, a, b, *more):
        return pl.pallas_call(
            next_kernel, out_shape=(*partial, *more), in_specs=[VMEM, VMEM, ANY, ANY],
            out_specs=(VMEM,) * (2 + len(more)),
            scratch_shapes=[
                *held, pltpu.VMEM((2 * RANK, n), BF16), pltpu.VMEM((n // LANES, RANK), F32), *sems,
            ],
            compiler_params=PARAMS, name=name,
        )(*wide, a, b)

    cosketch = total(*step("second", sketch, out_grads, acts))
    power = total(*step("third", cosketch, acts, out_grads))
    *project, left = step(
        "fourth", power, out_grads, acts, jax.ShapeDtypeStruct((rows, RANK), F32)
    )
    frozen, right = pl.pallas_call(
        last_kernel,
        out_shape=(
            jax.ShapeDtypeStruct((rows, cols), F32), jax.ShapeDtypeStruct((RANK, cols), F32),
        ),
        in_specs=[VMEM] * 4, out_specs=(VMEM, VMEM), compiler_params=PARAMS, name="last",
    )(*total(*project), left, weight)
    return (frozen, left, right)


def solution(mesh):
    mesh = Mesh(mesh.devices.reshape(4, 4, 2, 4), ("y", "x", "core", "z"))
    row = ("y", "x", "core")
    tokens = P((*row, "z"), None)
    return jax.shard_map(
        local, mesh=mesh, in_specs=(tokens, tokens, P(), P(row, "z")),
        out_specs=(P(row, "z"), P(row, None), P(None, "z")), check_vma=False,
    )
```

```python
import math

import jax
import jax.numpy as jnp
from jax import lax
from jax.experimental import pallas as pl
from jax.experimental.pallas import tpu as pltpu
from jax.sharding import Mesh, PartitionSpec as P

CHIPS = ("y", "x", "z")
F32 = jnp.float32
BF16 = jnp.bfloat16
RANK = 64
VMEM = pl.BlockSpec(memory_space=pltpu.VMEM)
HBM = pl.BlockSpec(memory_space=pltpu.HBM)
PARAMS = pltpu.CompilerParams(vmem_limit_bytes=16 * 2**20)
GROUPS = 4
LANES = 16


def dot(left, right, contract):
    dims = (((contract[0],), (contract[1],)), ((), ()))
    return lax.dot_general(left, right, dims, preferred_element_type=F32)


def split(value):
    high = value.astype(BF16)
    return high, (value - high.astype(F32)).astype(BF16)


def exact(left, right):
    left_high, left_low = split(left)
    right_high, right_low = split(right)
    return dot(
        jnp.concatenate([left_high, left_high, left_low], 1),
        jnp.concatenate([right_high, right_low, right_high], 0),
        (1, 0),
    )


def inverse_factor(gram):
    shape = (RANK, RANK)
    eye = lax.broadcasted_iota(jnp.int32, shape, 0) == lax.broadcasted_iota(jnp.int32, shape, 1)
    both = jnp.concatenate([gram, eye.astype(F32)], 1)
    work = [both[8 * i : 8 * i + 8] for i in range(8)]
    tile = (8, 2 * RANK)
    sub = lax.broadcasted_iota(jnp.int32, tile, 0)
    done = []
    for p in range(8):
        cols = {
            i: [jnp.broadcast_to(work[i][:, k : k + 1], tile) for k in range(8 * p, 8 * p + 8)]
            for i in range(p, 8)
        }
        pivots = jnp.zeros(tile, F32)
        for j in range(8):
            pivot = jnp.broadcast_to(cols[p][j][j : j + 1], tile)
            inverse = 1.0 / pivot
            pivots = jnp.where(sub == j, pivot, pivots)
            row = jnp.broadcast_to(work[p][j : j + 1], tile)
            ahead = {q: jnp.broadcast_to(cols[p][q][j : j + 1], tile) for q in range(j + 1, 8)}
            for i in range(p, 8):
                scale = cols[i][j] * inverse
                if i == p:
                    scale = jnp.where(sub > j, scale, 0.0)
                work[i] = work[i] - scale * row
                for q in range(j + 1, 8):
                    cols[i][q] = cols[i][q] - scale * ahead[q]
        done.append(work[p] * lax.rsqrt(pivots))
    return jnp.concatenate(done, 0)[:, RANK:]


def wide_block(first, own_ref, other_ref, lane):
    own = [own_ref[g * LANES + lane].astype(F32) for g in range(GROUPS)]
    other = [other_ref[g * LANES + lane].astype(F32) for g in range(GROUPS)]
    low = [jnp.where(first, a, b) for a, b in zip(own, other)]
    high = [jnp.where(first, b, a) for a, b in zip(own, other)]
    return jnp.concatenate(low + high, 0)


def gram_of(first, own_ref, other_ref, split_ref=None):
    width = own_ref.shape[2]
    gram = jnp.zeros((2 * RANK, 2 * RANK), F32)
    for lane in range(LANES):
        terms = jnp.concatenate(split(wide_block(first, own_ref, other_ref, lane)), 0)
        if split_ref is not None:
            split_ref[:, lane * width : (lane + 1) * width] = terms
        gram = gram + dot(terms, terms, (1, 1))
    cross = gram[:RANK, RANK:] + gram[RANK:, :RANK]
    return gram[:RANK, :RANK] + (gram[RANK:, RANK:] + cross)


def store_parts(first, part, index, keep_ref, send_ref):
    width = keep_ref.shape[2]
    for h in range(2):
        for g in range(GROUPS):
            low = part[8 * g : 8 * g + 8, h * width : (h + 1) * width]
            high = part[32 + 8 * g : 40 + 8 * g, h * width : (h + 1) * width]
            at = g * LANES + 2 * index + h
            keep_ref[at] = jnp.where(first, low, high)
            send_ref[at] = jnp.where(first, high, low).astype(BF16)


def chunks(total, size):
    return [(s, min(size, total - s)) for s in range(0, total, size)]


def row_copies(ref, held, sems):
    return [
        pltpu.make_async_copy(ref.at[pl.ds(s, n), :], held.at[pl.ds(s, n), :], sems.at[i])
        for i, (s, n) in enumerate(chunks(ref.shape[0], 256))
    ]


def col_copies(ref, held, sems):
    return [
        pltpu.make_async_copy(ref.at[:, pl.ds(s, n)], held.at[:, pl.ds(s, n)], sems.at[i])
        for i, (s, n) in enumerate(chunks(ref.shape[1], ref.shape[1] // 8))
    ]


def first_kernel(
    test_ref, a_ref, b_ref, keep_ref, send_ref, a_held, b_held, test_held, a_sems, b_sems, test_sem
):
    first = lax.axis_index("core") == 0
    test_copy = pltpu.make_async_copy(test_ref, test_held, test_sem)
    a_copies = row_copies(a_ref, a_held, a_sems)
    b_copies = col_copies(b_ref, b_held, b_sems)
    a_chunks = chunks(a_ref.shape[0], 256)
    b_chunks = chunks(b_ref.shape[1], b_ref.shape[1] // 8)
    for copy in [test_copy, *a_copies]:
        copy.start()
    test_copy.wait()
    test = test_held[...]
    applied = []
    for i, (copy, (s, n)) in enumerate(zip(a_copies, a_chunks)):
        copy.wait()
        for later in b_copies[2 * i : 2 * i + 2]:
            later.start()
        applied.append(dot(test, a_held[s : s + n, :], (1, 1)).astype(BF16))
    applied = jnp.concatenate(applied, 1)
    for i, (copy, (s, n)) in enumerate(zip(b_copies, b_chunks)):
        copy.wait()
        store_parts(first, dot(applied, b_held[:, s : s + n], (1, 0)), i, keep_ref, send_ref)


def next_kernel(own_ref, other_ref, a_ref, b_ref, keep_ref, send_ref, *rest):
    *left_ref, split_held = rest
    first = lax.axis_index("core") == 0
    gram = gram_of(first, own_ref, other_ref, split_held)
    inverse = inverse_factor(gram)
    raw = dot(split_held[...], a_ref[...], (1, 1))
    applied = exact(inverse, raw[:RANK] + raw[RANK:]).astype(BF16)
    for i, (s, n) in enumerate(chunks(b_ref.shape[1], b_ref.shape[1] // 8)):
        store_parts(first, dot(applied, b_ref[:, s : s + n], (1, 0)), i, keep_ref, send_ref)
    if left_ref:
        (left_ref,) = left_ref
        lane = lax.axis_index("y") * 4 + lax.axis_index("x")
        rows = left_ref.shape[1]
        left = exact(inverse, wide_block(first, own_ref, other_ref, lane))
        left = jnp.where(first, left[:, :rows], left[:, rows:])
        left_ref[...] = left * math.sqrt(a_ref.shape[1])


def last_kernel(own_ref, other_ref, left_ref, weight_ref, frozen_ref, left_out, right_ref):
    first = lax.axis_index("core") == 0
    inverse = inverse_factor(gram_of(first, own_ref, other_ref))
    width = own_ref.shape[2]
    left_out[...] = left_ref[...]
    left = left_ref[...].T
    for q in range(4):
        block = wide_block(first, own_ref, other_ref, lax.axis_index("z") * 4 + q)
        right = exact(inverse, block) * math.sqrt(LANES * width)
        at = slice(q * width, (q + 1) * width)
        right_ref[:, at] = right
        frozen_ref[:, at] = weight_ref[:, at].astype(F32) - exact(left, right) / math.sqrt(RANK)


def in_hbm(array):
    return pltpu.with_memory_space_constraint(array, pltpu.HBM)


def in_vmem(array):
    return pltpu.with_memory_space_constraint(array, pltpu.VMEM)


def total(keep, send, dtype=F32):
    got = lax.ppermute(send, "core", [(0, 1), (1, 0)])
    pair = (keep + got.astype(F32)).astype(BF16)
    terms = lax.all_to_all(pair, CHIPS, 0, 0, tiled=True)
    mine = lax.optimization_barrier(jnp.sum(terms.astype(F32), axis=0)).astype(dtype)
    copies = jnp.broadcast_to(mine[None], terms.shape)
    own = lax.all_to_all(copies, CHIPS, 0, 0, tiled=True)
    return own, lax.ppermute(own, "core", [(0, 1), (1, 0)])


def local(acts, out_grads, test_matrix, weight):
    tokens, n = acts.shape
    rows, cols = weight.shape
    parts = (LANES * GROUPS, 8, n // LANES)
    partial = (jax.ShapeDtypeStruct(parts, F32), jax.ShapeDtypeStruct(parts, BF16))
    held = pltpu.VMEM((tokens, n), BF16)
    keep, send, acts, out_grads = pl.pallas_call(
        first_kernel, out_shape=(*partial, held, held), in_specs=[HBM] * 3,
        out_specs=(VMEM,) * 4,
        scratch_shapes=[
            pltpu.VMEM((RANK, n), BF16), pltpu.SemaphoreType.DMA((len(chunks(tokens, 256)),)),
            pltpu.SemaphoreType.DMA((8,)), pltpu.SemaphoreType.DMA(()),
        ],
        compiler_params=PARAMS, name="first",
    )(in_hbm(test_matrix.T), in_hbm(acts), in_hbm(out_grads))

    def step(name, wide, a, b, *more):
        return pl.pallas_call(
            next_kernel, out_shape=(*partial, *more), in_specs=[VMEM] * 4,
            out_specs=(VMEM,) * (2 + len(more)),
            scratch_shapes=[pltpu.VMEM((2 * RANK, n), BF16)],
            compiler_params=PARAMS, name=name,
        )(*wide, in_vmem(a), in_vmem(b))

    sketch = total(keep, send)
    cosketch = total(*step("second", sketch, out_grads, acts), BF16)
    power = total(*step("third", cosketch, acts, out_grads))
    *project, left = step(
        "fourth", power, out_grads, acts, pltpu.VMEM((RANK, rows), F32)
    )
    frozen, left, right = pl.pallas_call(
        last_kernel,
        out_shape=(
            jax.ShapeDtypeStruct((rows, cols), F32), jax.ShapeDtypeStruct((RANK, rows), F32),
            jax.ShapeDtypeStruct((RANK, cols), F32),
        ),
        in_specs=[VMEM] * 4, out_specs=(VMEM,) * 3, compiler_params=PARAMS, name="last",
    )(*total(*project), left, weight)
    return (frozen, left.T, right)


def solution(mesh):
    mesh = Mesh(mesh.devices.reshape(4, 4, 2, 4), ("y", "x", "core", "z"))
    row = ("y", "x", "core")
    tokens = P((*row, "z"), None)
    return jax.shard_map(
        local, mesh=mesh, in_specs=(tokens, tokens, P(), P(row, "z")),
        out_specs=(P(row, "z"), P(row, None), P(None, "z")), check_vma=False,
    )
```

```python
import math

import jax
import jax.numpy as jnp
from jax import lax
from jax.experimental import pallas as pl
from jax.experimental.pallas import tpu as pltpu
from jax.sharding import Mesh, PartitionSpec as P

CHIPS = ("y", "x", "z")
F32 = jnp.float32
BF16 = jnp.bfloat16
RANK = 64
VMEM = pl.BlockSpec(memory_space=pltpu.VMEM)
HBM = pl.BlockSpec(memory_space=pltpu.HBM)
PARAMS = pltpu.CompilerParams(vmem_limit_bytes=16 * 2**20)
AHEAD = 3
GROUPS = 8
LANES = 8


def dot(left, right, contract):
    dims = (((contract[0],), (contract[1],)), ((), ()))
    return lax.dot_general(left, right, dims, preferred_element_type=F32)


def split(value):
    high = value.astype(BF16)
    return high, (value - high.astype(F32)).astype(BF16)


def exact(left, right):
    left_high, left_low = split(left)
    right_high, right_low = split(right)
    return dot(
        jnp.concatenate([left_high, left_high, left_low], 1),
        jnp.concatenate([right_high, right_low, right_high], 0),
        (1, 0),
    )


def inverse_factor(gram):
    shape = (RANK, RANK)
    eye = lax.broadcasted_iota(jnp.int32, shape, 0) == lax.broadcasted_iota(jnp.int32, shape, 1)
    both = jnp.concatenate([gram, eye.astype(F32)], 1)
    work = [both[8 * i : 8 * i + 8] for i in range(8)]
    tile = (8, 2 * RANK)
    sub = lax.broadcasted_iota(jnp.int32, tile, 0)
    done = []
    for p in range(8):
        cols = {
            i: [jnp.broadcast_to(work[i][:, k : k + 1], tile) for k in range(8 * p, 8 * p + 8)]
            for i in range(p, 8)
        }
        pivots = jnp.zeros(tile, F32)
        for j in range(8):
            pivot = jnp.broadcast_to(cols[p][j][j : j + 1], tile)
            inverse = 1.0 / pivot
            pivots = jnp.where(sub == j, pivot, pivots)
            row = jnp.broadcast_to(work[p][j : j + 1], tile)
            ahead = {q: jnp.broadcast_to(cols[p][q][j : j + 1], tile) for q in range(j + 1, 8)}
            for i in range(p, 8):
                scale = cols[i][j] * inverse
                if i == p:
                    scale = jnp.where(sub > j, scale, 0.0)
                work[i] = work[i] - scale * row
                for q in range(j + 1, 8):
                    cols[i][q] = cols[i][q] - scale * ahead[q]
        done.append(work[p] * lax.rsqrt(pivots))
    return jnp.concatenate(done, 0)[:, RANK:]


def wide_block(first, own_ref, other_ref, half, lane):
    swap = first if half == 0 else jnp.logical_not(first)
    own = jnp.concatenate([own_ref[g * LANES + lane].astype(F32) for g in range(GROUPS)], 0)
    other = jnp.concatenate([other_ref[g * LANES + lane].astype(F32) for g in range(GROUPS)], 0)
    return jnp.where(swap, own, other)


def gram_of(first, own_ref, other_ref, split_ref=None):
    width = own_ref.shape[2]
    gram = jnp.zeros((2 * RANK, 2 * RANK), F32)
    for half in range(2):
        for lane in range(LANES):
            block = wide_block(first, own_ref, other_ref, half, lane)
            terms = jnp.concatenate(split(block), 0)
            if split_ref is not None:
                start = (half * LANES + lane) * width
                split_ref[:, start : start + width] = terms
            gram = gram + dot(terms, terms, (1, 1))
    cross = gram[:RANK, RANK:] + gram[RANK:, :RANK]
    return gram[:RANK, :RANK] + (gram[RANK:, RANK:] + cross)


def half_columns(ref, half, index):
    size = ref.shape[1] // 8
    return pl.ds(pl.multiple_of(half * (4 * size) + index * size, size), size)


def store_parts(part, index, ref):
    width = ref.shape[2]
    for h in range(2):
        for g in range(GROUPS):
            value = part[8 * g : 8 * g + 8, h * width : (h + 1) * width]
            ref[g * LANES + 2 * index + h] = value.astype(ref.dtype)


def chunks(total, size):
    return [(s, min(size, total - s)) for s in range(0, total, size)]


def first_kernel(
    test_ref, a_ref, b_ref, send_ref, applied_ref, a_held, b_held, test_held, a_sems, b_sems, test_sem
):
    core = lax.axis_index("core")
    places = [half_columns(b_ref, half, i) for half in (1 - core, core) for i in range(4)]
    rows = chunks(a_ref.shape[0], 128)
    test_copy = pltpu.make_async_copy(test_ref, test_held, test_sem)
    copies = [
        pltpu.make_async_copy(a_ref.at[pl.ds(s, n), :], a_held.at[pl.ds(s, n), :], a_sems.at[i])
        for i, (s, n) in enumerate(rows)
    ] + [
        pltpu.make_async_copy(b_ref.at[:, at], b_held.at[:, at], b_sems.at[i])
        for i, at in enumerate(places)
    ]
    test_copy.start()
    for copy in copies[:AHEAD]:
        copy.start()
    test_copy.wait()

    def arrive(i):
        copies[i].wait()
        if i + AHEAD < len(copies):
            copies[i + AHEAD].start()

    test = test_held[...]
    applied = []
    for i in range(0, len(rows), 2):
        start = rows[i][0]
        stop = sum(rows[min(i + 1, len(rows) - 1)])
        for j in range(i, min(i + 2, len(rows))):
            arrive(j)
        applied.append(dot(test, a_held[start:stop, :], (1, 1)).astype(BF16))
    applied = jnp.concatenate(applied, 1)
    applied_ref[...] = applied
    for i, at in enumerate(places):
        arrive(len(rows) + i)
        if i < 4:
            store_parts(dot(applied, b_held[:, at], (1, 0)), i, send_ref)


def next_kernel(own_ref, other_ref, a_ref, b_ref, send_ref, applied_ref, inverse_ref, split_held):
    core = lax.axis_index("core")
    gram = gram_of(core == 0, own_ref, other_ref, split_held)
    inverse = inverse_factor(gram)
    inverse_ref[...] = inverse
    raw = dot(split_held[...], a_ref[...], (1, 1))
    applied = exact(inverse, raw[:RANK] + raw[RANK:]).astype(BF16)
    applied_ref[...] = applied
    for i in range(4):
        part = dot(applied, b_ref[:, half_columns(b_ref, 1 - core, i)], (1, 0))
        store_parts(part, i, send_ref)


def keep_kernel(applied_ref, b_ref, keep_ref):
    core = lax.axis_index("core")
    for i in range(4):
        part = dot(applied_ref[...], b_ref[:, half_columns(b_ref, core, i)], (1, 0))
        store_parts(part, i, keep_ref)


def left_kernel(own_ref, other_ref, inverse_ref, left_ref):
    core = lax.axis_index("core")
    block = 4 * lax.axis_index("y") + lax.axis_index("x")
    half, lane = block // LANES, lax.rem(block, LANES)
    wide = jnp.where(
        half == 0,
        wide_block(core == 0, own_ref, other_ref, 0, lane),
        wide_block(core == 0, own_ref, other_ref, 1, lane),
    )
    left = exact(inverse_ref[...], wide)
    rows = left_ref.shape[1]
    left = jnp.where(core == 0, left[:, :rows], left[:, rows:])
    left_ref[...] = left * math.sqrt(2 * LANES * own_ref.shape[2])


def last_kernel(own_ref, other_ref, left_ref, weight_ref, frozen_ref, left_out, right_ref):
    first = lax.axis_index("core") == 0
    inverse = inverse_factor(gram_of(first, own_ref, other_ref))
    width = own_ref.shape[2]
    left_out[...] = left_ref[...]
    left = left_ref[...].T
    half = lax.axis_index("z") // 2
    for q in range(4):
        lane = lax.rem(lax.axis_index("z"), 2) * 4 + q
        block = jnp.where(
            half == 0,
            wide_block(first, own_ref, other_ref, 0, lane),
            wide_block(first, own_ref, other_ref, 1, lane),
        )
        right = exact(inverse, block) * math.sqrt(2 * LANES * width)
        at = slice(q * width, (q + 1) * width)
        right_ref[:, at] = right
        frozen_ref[:, at] = weight_ref[:, at].astype(F32) - exact(left, right) / math.sqrt(RANK)


def in_hbm(array):
    return pltpu.with_memory_space_constraint(array, pltpu.HBM)


def in_vmem(array):
    return pltpu.with_memory_space_constraint(array, pltpu.VMEM)


def total(send, applied, b, dtype=F32):
    keep = pl.pallas_call(
        keep_kernel, out_shape=jax.ShapeDtypeStruct(send.shape, F32), in_specs=[VMEM] * 2,
        out_specs=VMEM, compiler_params=PARAMS, name="keep",
    )(applied, in_vmem(b))
    got = lax.ppermute(send, "core", [(0, 1), (1, 0)])
    pair = (keep + got.astype(F32)).astype(BF16)
    terms = lax.all_to_all(pair, CHIPS, 0, 0, tiled=True)
    mine = lax.optimization_barrier(jnp.sum(terms.astype(F32), axis=0)).astype(dtype)
    copies = jnp.broadcast_to(mine[None], terms.shape)
    own = lax.all_to_all(copies, CHIPS, 0, 0, tiled=True)
    return own, lax.ppermute(own, "core", [(0, 1), (1, 0)])


def local(acts, out_grads, test_matrix, weight):
    tokens, n = acts.shape
    rows, cols = weight.shape
    partial = (
        jax.ShapeDtypeStruct((LANES * GROUPS, 8, n // (2 * LANES)), BF16),
        jax.ShapeDtypeStruct((RANK, tokens), BF16),
    )
    held = pltpu.VMEM((tokens, n), BF16)
    *made, acts, out_grads = pl.pallas_call(
        first_kernel, out_shape=(*partial, held, held), in_specs=[HBM] * 3,
        out_specs=(VMEM,) * 4,
        scratch_shapes=[
            pltpu.VMEM((RANK, n), BF16), pltpu.SemaphoreType.DMA((len(chunks(tokens, 128)),)),
            pltpu.SemaphoreType.DMA((8,)), pltpu.SemaphoreType.DMA(()),
        ],
        compiler_params=PARAMS, name="first",
    )(in_hbm(test_matrix.T), in_hbm(acts), in_hbm(out_grads))

    def step(wide, a, b):
        return pl.pallas_call(
            next_kernel, out_shape=(*partial, jax.ShapeDtypeStruct((RANK, RANK), F32)),
            in_specs=[VMEM] * 4, out_specs=(VMEM,) * 3,
            scratch_shapes=[pltpu.VMEM((2 * RANK, n), BF16)], compiler_params=PARAMS, name="step",
        )(*wide, in_vmem(a), in_vmem(b))

    sketch = total(*made, out_grads)
    *made, _ = step(sketch, out_grads, acts)
    cosketch = total(*made, acts, BF16)
    *made, _ = step(cosketch, acts, out_grads)
    power = total(*made, out_grads)
    *made, inverse = step(power, out_grads, acts)
    left = pl.pallas_call(
        left_kernel, out_shape=pltpu.VMEM((RANK, rows), F32), in_specs=[VMEM] * 3, out_specs=VMEM,
        compiler_params=PARAMS, name="left",
    )(*power, inverse)
    frozen, left, right = pl.pallas_call(
        last_kernel,
        out_shape=(
            jax.ShapeDtypeStruct((rows, cols), F32), jax.ShapeDtypeStruct((RANK, rows), F32),
            jax.ShapeDtypeStruct((RANK, cols), F32),
        ),
        in_specs=[VMEM] * 4, out_specs=(VMEM,) * 3, compiler_params=PARAMS, name="last",
    )(*total(*made, acts), left, weight)
    return (frozen, left.T, right)


def solution(mesh):
    mesh = Mesh(mesh.devices.reshape(4, 4, 2, 4), ("y", "x", "core", "z"))
    row = ("y", "x", "core")
    tokens = P((*row, "z"), None)
    return jax.shard_map(
        local, mesh=mesh, in_specs=(tokens, tokens, P(), P(row, "z")),
        out_specs=(P(row, "z"), P(row, None), P(None, "z")), check_vma=False,
    )
```

```python
import math

import jax
import jax.numpy as jnp
from jax import lax
from jax.experimental import pallas as pl
from jax.experimental.pallas import tpu as pltpu
from jax.sharding import Mesh, PartitionSpec as P

CHIPS = ("y", "x", "z")
F32 = jnp.float32
BF16 = jnp.bfloat16
RANK = 64
VMEM = pl.BlockSpec(memory_space=pltpu.VMEM)
HBM = pl.BlockSpec(memory_space=pltpu.HBM)
PARAMS = pltpu.CompilerParams(vmem_limit_bytes=16 * 2**20)
GROUPS = 8
LANES = 8


def dot(left, right, contract):
    dims = (((contract[0],), (contract[1],)), ((), ()))
    return lax.dot_general(left, right, dims, preferred_element_type=F32)


def split(value):
    high = value.astype(BF16)
    return high, (value - high.astype(F32)).astype(BF16)


def exact(left, right):
    left_high, left_low = split(left)
    right_high, right_low = split(right)
    return dot(
        jnp.concatenate([left_high, left_high, left_low], 1),
        jnp.concatenate([right_high, right_low, right_high], 0),
        (1, 0),
    )


def inverse_factor(gram):
    shape = (RANK, RANK)
    eye = lax.broadcasted_iota(jnp.int32, shape, 0) == lax.broadcasted_iota(jnp.int32, shape, 1)
    both = jnp.concatenate([gram, eye.astype(F32)], 1)
    work = [both[8 * i : 8 * i + 8] for i in range(8)]
    tile = (8, 2 * RANK)
    sub = lax.broadcasted_iota(jnp.int32, tile, 0)
    done = []
    for p in range(8):
        cols = {
            i: [jnp.broadcast_to(work[i][:, k : k + 1], tile) for k in range(8 * p, 8 * p + 8)]
            for i in range(p, 8)
        }
        pivots = jnp.zeros(tile, F32)
        for j in range(8):
            pivot = jnp.broadcast_to(cols[p][j][j : j + 1], tile)
            inverse = 1.0 / pivot
            pivots = jnp.where(sub == j, pivot, pivots)
            row = jnp.broadcast_to(work[p][j : j + 1], tile)
            ahead = {q: jnp.broadcast_to(cols[p][q][j : j + 1], tile) for q in range(j + 1, 8)}
            for i in range(p, 8):
                scale = cols[i][j] * inverse
                if i == p:
                    scale = jnp.where(sub > j, scale, 0.0)
                work[i] = work[i] - scale * row
                for q in range(j + 1, 8):
                    cols[i][q] = cols[i][q] - scale * ahead[q]
        done.append(work[p] * lax.rsqrt(pivots))
    return jnp.concatenate(done, 0)[:, RANK:]


def wide_block(first, own_ref, other_ref, half, lane):
    swap = first if half == 0 else jnp.logical_not(first)
    own = jnp.concatenate([own_ref[g * LANES + lane].astype(F32) for g in range(GROUPS)], 0)
    other = jnp.concatenate([other_ref[g * LANES + lane].astype(F32) for g in range(GROUPS)], 0)
    return jnp.where(swap, own, other)


def half_gram(ref, split_ref=None):
    width = ref.shape[2]
    gram = jnp.zeros((2 * RANK, 2 * RANK), F32)
    for lane in range(LANES):
        block = jnp.concatenate([ref[g * LANES + lane].astype(F32) for g in range(GROUPS)], 0)
        terms = jnp.concatenate(split(block), 0)
        if split_ref is not None:
            split_ref[:, lane * width : (lane + 1) * width] = terms
        gram = gram + dot(terms, terms, (1, 1))
    return gram


def whole_gram(gram):
    cross = gram[:RANK, RANK:] + gram[RANK:, :RANK]
    return gram[:RANK, :RANK] + (gram[RANK:, RANK:] + cross)


def half_product(terms, ref, half):
    size = ref.shape[1] // 2
    raw = dot(terms, ref[:, pl.ds(pl.multiple_of(half * size, size), size)], (1, 1))
    return raw[:RANK] + raw[RANK:]


def half_columns(ref, half, index):
    size = ref.shape[1] // 8
    return pl.ds(pl.multiple_of(half * (4 * size) + index * size, size), size)


def store_parts(part, index, ref):
    width = ref.shape[2]
    for h in range(2):
        for g in range(GROUPS):
            value = part[8 * g : 8 * g + 8, h * width : (h + 1) * width]
            ref[g * LANES + 2 * index + h] = value.astype(ref.dtype)


def chunks(total, size):
    return [(s, min(size, total - s)) for s in range(0, total, size)]


def first_kernel(
    test_ref, a_ref, b_ref, send_ref, applied_ref, a_held, b_held, test_held, a_sems, b_sems, test_sem
):
    core = lax.axis_index("core")
    places = [half_columns(b_ref, half, i) for half in (1 - core, core) for i in range(4)]
    rows = chunks(a_ref.shape[0], 256)
    test_copy = pltpu.make_async_copy(test_ref, test_held, test_sem)
    a_copies = [
        pltpu.make_async_copy(a_ref.at[pl.ds(s, n), :], a_held.at[pl.ds(s, n), :], a_sems.at[i])
        for i, (s, n) in enumerate(rows)
    ]
    b_copies = [
        pltpu.make_async_copy(b_ref.at[:, at], b_held.at[:, at], b_sems.at[i])
        for i, at in enumerate(places)
    ]
    for copy in [test_copy, *a_copies]:
        copy.start()
    test_copy.wait()
    test = test_held[...]
    applied = []
    for i, (copy, (s, n)) in enumerate(zip(a_copies, rows)):
        copy.wait()
        for later in b_copies[4 * i : 4 * i + 4]:
            later.start()
        applied.append(dot(test, a_held[s : s + n, :], (1, 1)).astype(BF16))
    applied = jnp.concatenate(applied, 1)
    applied_ref[...] = applied
    for copy in b_copies[:4]:
        copy.wait()
    for i in range(4):
        store_parts(dot(applied, b_held[:, places[i]], (1, 0)), i, send_ref)
    for copy in b_copies[4:]:
        copy.wait()


def own_kernel(own_ref, a_ref, gram_ref, raw_ref, split_held):
    gram_ref[...] = half_gram(own_ref, split_held)
    raw_ref[...] = half_product(split_held[...], a_ref, lax.axis_index("core"))


def own_gram_kernel(own_ref, gram_ref):
    gram_ref[...] = half_gram(own_ref)


def next_kernel(
    other_ref, gram_ref, raw_ref, a_ref, b_ref, send_ref, applied_ref, inverse_ref, split_held
):
    other = 1 - lax.axis_index("core")
    inverse = inverse_factor(whole_gram(gram_ref[...] + half_gram(other_ref, split_held)))
    inverse_ref[...] = inverse
    raw = raw_ref[...] + half_product(split_held[...], a_ref, other)
    applied = exact(inverse, raw).astype(BF16)
    applied_ref[...] = applied
    for i in range(4):
        part = dot(applied, b_ref[:, half_columns(b_ref, other, i)], (1, 0))
        store_parts(part, i, send_ref)


def keep_kernel(applied_ref, b_ref, keep_ref):
    core = lax.axis_index("core")
    for i in range(4):
        part = dot(applied_ref[...], b_ref[:, half_columns(b_ref, core, i)], (1, 0))
        store_parts(part, i, keep_ref)


def left_kernel(own_ref, other_ref, inverse_ref, left_ref):
    core = lax.axis_index("core")
    block = 4 * lax.axis_index("y") + lax.axis_index("x")
    half, lane = block // LANES, lax.rem(block, LANES)
    wide = jnp.where(
        half == 0,
        wide_block(core == 0, own_ref, other_ref, 0, lane),
        wide_block(core == 0, own_ref, other_ref, 1, lane),
    )
    left = exact(inverse_ref[...], wide)
    rows = left_ref.shape[1]
    left = jnp.where(core == 0, left[:, :rows], left[:, rows:])
    left_ref[...] = left * math.sqrt(2 * LANES * own_ref.shape[2])


def last_kernel(
    own_ref, other_ref, gram_ref, left_ref, weight_ref, frozen_ref, left_out, right_ref
):
    first = lax.axis_index("core") == 0
    inverse = inverse_factor(whole_gram(gram_ref[...] + half_gram(other_ref)))
    width = own_ref.shape[2]
    left_out[...] = left_ref[...]
    left = left_ref[...].T
    half = lax.axis_index("z") // 2
    for q in range(4):
        lane = lax.rem(lax.axis_index("z"), 2) * 4 + q
        block = jnp.where(
            half == 0,
            wide_block(first, own_ref, other_ref, 0, lane),
            wide_block(first, own_ref, other_ref, 1, lane),
        )
        right = exact(inverse, block) * math.sqrt(2 * LANES * width)
        at = slice(q * width, (q + 1) * width)
        right_ref[:, at] = right
        frozen_ref[:, at] = weight_ref[:, at].astype(F32) - exact(left, right) / math.sqrt(RANK)


def in_hbm(array):
    return pltpu.with_memory_space_constraint(array, pltpu.HBM)


def in_vmem(array):
    return pltpu.with_memory_space_constraint(array, pltpu.VMEM)


def total(send, applied, b, dtype=F32):
    keep = pl.pallas_call(
        keep_kernel, out_shape=jax.ShapeDtypeStruct(send.shape, F32), in_specs=[VMEM] * 2,
        out_specs=VMEM, compiler_params=PARAMS, name="keep",
    )(applied, in_vmem(b))
    got = lax.ppermute(send, "core", [(0, 1), (1, 0)])
    pair = (keep + got.astype(F32)).astype(BF16)
    terms = lax.all_to_all(pair, CHIPS, 0, 0, tiled=True)
    mine = lax.optimization_barrier(jnp.sum(terms.astype(F32), axis=0)).astype(dtype)
    copies = jnp.broadcast_to(mine[None], terms.shape)
    own = lax.all_to_all(copies, CHIPS, 0, 0, tiled=True)
    return own, lax.ppermute(own, "core", [(0, 1), (1, 0)])


def local(acts, out_grads, test_matrix, weight):
    tokens, n = acts.shape
    rows, cols = weight.shape
    partial = (
        jax.ShapeDtypeStruct((LANES * GROUPS, 8, n // (2 * LANES)), BF16),
        jax.ShapeDtypeStruct((RANK, tokens), BF16),
    )
    held = pltpu.VMEM((tokens, n), BF16)
    *made, acts, out_grads = pl.pallas_call(
        first_kernel, out_shape=(*partial, held, held), in_specs=[HBM] * 3,
        out_specs=(VMEM,) * 4,
        scratch_shapes=[
            pltpu.VMEM((RANK, n), BF16), pltpu.SemaphoreType.DMA((len(chunks(tokens, 256)),)),
            pltpu.SemaphoreType.DMA((8,)), pltpu.SemaphoreType.DMA(()),
        ],
        compiler_params=PARAMS, name="first",
    )(in_hbm(test_matrix.T), in_hbm(acts), in_hbm(out_grads))

    gram = jax.ShapeDtypeStruct((2 * RANK, 2 * RANK), F32)

    def step(wide, a, b):
        own, other = wide
        raw = jax.ShapeDtypeStruct((RANK, tokens), F32)
        terms = pltpu.VMEM((2 * RANK, n // 2), BF16)
        sums = pl.pallas_call(
            own_kernel, out_shape=(gram, raw), in_specs=[VMEM] * 2, out_specs=(VMEM,) * 2,
            scratch_shapes=[terms], compiler_params=PARAMS, name="own",
        )(own, in_vmem(a))
        return pl.pallas_call(
            next_kernel, out_shape=(*partial, jax.ShapeDtypeStruct((RANK, RANK), F32)),
            in_specs=[VMEM] * 5, out_specs=(VMEM,) * 3, scratch_shapes=[terms],
            compiler_params=PARAMS, name="step",
        )(other, *sums, in_vmem(a), in_vmem(b))

    sketch = total(*made, out_grads)
    *made, _ = step(sketch, out_grads, acts)
    cosketch = total(*made, acts, BF16)
    *made, _ = step(cosketch, acts, out_grads)
    power = total(*made, out_grads)
    *made, inverse = step(power, out_grads, acts)
    left = pl.pallas_call(
        left_kernel, out_shape=pltpu.VMEM((RANK, rows), F32), in_specs=[VMEM] * 3, out_specs=VMEM,
        compiler_params=PARAMS, name="left",
    )(*power, inverse)
    own, other = total(*made, acts)
    own_gram = pl.pallas_call(
        own_gram_kernel, out_shape=gram, in_specs=[VMEM], out_specs=VMEM, compiler_params=PARAMS,
        name="own_gram",
    )(own)
    frozen, left, right = pl.pallas_call(
        last_kernel,
        out_shape=(
            jax.ShapeDtypeStruct((rows, cols), F32), jax.ShapeDtypeStruct((RANK, rows), F32),
            jax.ShapeDtypeStruct((RANK, cols), F32),
        ),
        in_specs=[VMEM] * 5, out_specs=(VMEM,) * 3, compiler_params=PARAMS, name="last",
    )(own, other, own_gram, left, weight)
    return (frozen, left.T, right)


def solution(mesh):
    mesh = Mesh(mesh.devices.reshape(4, 4, 2, 4), ("y", "x", "core", "z"))
    row = ("y", "x", "core")
    tokens = P((*row, "z"), None)
    return jax.shard_map(
        local, mesh=mesh, in_specs=(tokens, tokens, P(), P(row, "z")),
        out_specs=(P(row, "z"), P(row, None), P(None, "z")), check_vma=False,
    )
```

```python
import math

import jax
import jax.numpy as jnp
from jax import lax
from jax.experimental import pallas as pl
from jax.experimental.pallas import tpu as pltpu
from jax.sharding import Mesh, PartitionSpec as P

CHIPS = ("yh", "z", "yl", "x")
F32 = jnp.float32
BF16 = jnp.bfloat16
RANK = 64
VMEM = pl.BlockSpec(memory_space=pltpu.VMEM)
HBM = pl.BlockSpec(memory_space=pltpu.HBM)
PARAMS = pltpu.CompilerParams(vmem_limit_bytes=16 * 2**20)
GROUPS = 8
LANES = 8
TILES = 3
TILE = 128


def dot(left, right, contract):
    dims = (((contract[0],), (contract[1],)), ((), ()))
    return lax.dot_general(left, right, dims, preferred_element_type=F32)


def split(value):
    high = value.astype(BF16)
    return high, (value - high.astype(F32)).astype(BF16)


def exact(left, right):
    left_high, left_low = split(left)
    right_high, right_low = split(right)
    return dot(
        jnp.concatenate([left_high, left_high, left_low], 1),
        jnp.concatenate([right_high, right_low, right_high], 0),
        (1, 0),
    )


def inverse_factor(gram):
    shape = (RANK, RANK)
    eye = lax.broadcasted_iota(jnp.int32, shape, 0) == lax.broadcasted_iota(jnp.int32, shape, 1)
    both = jnp.concatenate([gram, eye.astype(F32)], 1)
    work = [both[8 * i : 8 * i + 8] for i in range(8)]
    tile = (8, 2 * RANK)
    sub = lax.broadcasted_iota(jnp.int32, tile, 0)
    done = []
    for p in range(8):
        cols = {
            i: [jnp.broadcast_to(work[i][:, k : k + 1], tile) for k in range(8 * p, 8 * p + 8)]
            for i in range(p, 8)
        }
        pivots = jnp.zeros(tile, F32)
        for j in range(8):
            pivot = jnp.broadcast_to(cols[p][j][j : j + 1], tile)
            inverse = 1.0 / pivot
            pivots = jnp.where(sub == j, pivot, pivots)
            row = jnp.broadcast_to(work[p][j : j + 1], tile)
            ahead = {q: jnp.broadcast_to(cols[p][q][j : j + 1], tile) for q in range(j + 1, 8)}
            for i in range(p, 8):
                scale = cols[i][j] * inverse
                if i == p:
                    scale = jnp.where(sub > j, scale, 0.0)
                work[i] = work[i] - scale * row
                for q in range(j + 1, 8):
                    cols[i][q] = cols[i][q] - scale * ahead[q]
        done.append(work[p] * lax.rsqrt(pivots))
    return jnp.concatenate(done, 0)[:, RANK:]


def lane_of(block, tile):
    return (block - tile + LANES) % LANES


def block_of(ref, block, low=False):
    def tile(g, j):
        at = g * LANES + lane_of(block, j)
        value = ref[at, j].astype(F32)
        return value + ref[at, TILES].astype(F32) if low else value

    rows = [jnp.concatenate([tile(g, j) for j in range(TILES)], 1) for g in range(GROUPS)]
    return jnp.concatenate(rows, 0)


def half_gram(ref, split_ref=None):
    width = TILES * TILE
    gram = jnp.zeros((2 * RANK, 2 * RANK), F32)
    for block in range(LANES):
        terms = jnp.concatenate(split(block_of(ref, block)), 0)
        if split_ref is not None:
            split_ref[:, block * width : (block + 1) * width] = terms
        gram = gram + dot(terms, terms, (1, 1))
    return gram


def whole_gram(gram):
    cross = gram[:RANK, RANK:] + gram[RANK:, :RANK]
    return gram[:RANK, :RANK] + (gram[RANK:, RANK:] + cross)


def half_product(terms, ref, half):
    size = ref.shape[1] // 2
    raw = dot(terms, ref[:, pl.ds(pl.multiple_of(half * size, size), size)], (1, 1))
    return raw[:RANK] + raw[RANK:]


def half_columns(ref, half, index):
    size = ref.shape[1] // 8
    return pl.ds(pl.multiple_of(half * (4 * size) + index * size, size), size)


def store_parts(part, index, ref):
    for h in range(2):
        for g in range(GROUPS):
            for j in range(TILES):
                start = (h * TILES + j) * TILE
                value = part[8 * g : 8 * g + 8, start : start + TILE]
                ref[g * LANES + lane_of(2 * index + h, j), j] = value.astype(ref.dtype)


def chunks(total, size):
    return [(s, min(size, total - s)) for s in range(0, total, size)]


def first_kernel(
    test_ref, a_ref, b_ref, send_ref, applied_ref, a_held, b_held, test_held, a_sems, b_sems, test_sem
):
    core = lax.axis_index("core")
    places = [half_columns(b_ref, half, i) for half in (1 - core, core) for i in range(4)]
    rows = chunks(a_ref.shape[0], 256)
    test_copy = pltpu.make_async_copy(test_ref, test_held, test_sem)
    a_copies = [
        pltpu.make_async_copy(a_ref.at[pl.ds(s, n), :], a_held.at[pl.ds(s, n), :], a_sems.at[i])
        for i, (s, n) in enumerate(rows)
    ]
    b_copies = [
        pltpu.make_async_copy(b_ref.at[:, at], b_held.at[:, at], b_sems.at[i])
        for i, at in enumerate(places)
    ]
    for copy in [test_copy, *a_copies]:
        copy.start()
    test_copy.wait()
    test = test_held[...]
    applied = []
    for i, (copy, (s, n)) in enumerate(zip(a_copies, rows)):
        copy.wait()
        for later in b_copies[4 * i : 4 * i + 4]:
            later.start()
        applied.append(dot(test, a_held[s : s + n, :], (1, 1)).astype(BF16))
    applied = jnp.concatenate(applied, 1)
    applied_ref[...] = applied
    for copy in b_copies[:4]:
        copy.wait()
    for i in range(4):
        store_parts(dot(applied, b_held[:, places[i]], (1, 0)), i, send_ref)
    for copy in b_copies[4:]:
        copy.wait()


def own_kernel(own_ref, a_ref, gram_ref, raw_ref, split_held):
    gram_ref[...] = half_gram(own_ref, split_held)
    raw_ref[...] = half_product(split_held[...], a_ref, lax.axis_index("core"))


def own_gram_kernel(own_ref, gram_ref):
    gram_ref[...] = half_gram(own_ref)


def next_kernel(
    other_ref, gram_ref, raw_ref, a_ref, b_ref, send_ref, applied_ref, inverse_ref, split_held
):
    other = 1 - lax.axis_index("core")
    inverse = inverse_factor(whole_gram(gram_ref[...] + half_gram(other_ref, split_held)))
    inverse_ref[...] = inverse
    raw = raw_ref[...] + half_product(split_held[...], a_ref, other)
    applied = exact(inverse, raw).astype(BF16)
    applied_ref[...] = applied
    for i in range(4):
        part = dot(applied, b_ref[:, half_columns(b_ref, other, i)], (1, 0))
        store_parts(part, i, send_ref)


def keep_kernel(applied_ref, b_ref, keep_ref):
    core = lax.axis_index("core")
    for i in range(4):
        part = dot(applied_ref[...], b_ref[:, half_columns(b_ref, core, i)], (1, 0))
        store_parts(part, i, keep_ref)


def left_kernel(own_ref, other_ref, inverse_ref, left_ref):
    core = lax.axis_index("core")
    block = 4 * lax.axis_index("yl") + lax.axis_index("x")
    wide = jnp.where(
        core == lax.axis_index("yh"),
        block_of(own_ref, block, low=True),
        block_of(other_ref, block, low=True),
    )
    left = exact(inverse_ref[...], wide)
    rows = left_ref.shape[1]
    left = jnp.where(core == 0, left[:, :rows], left[:, rows:])
    left_ref[...] = left * math.sqrt(2 * LANES * TILES * TILE)


def last_kernel(
    own_ref, other_ref, gram_ref, left_ref, weight_ref, frozen_ref, left_out, right_ref
):
    core, z = lax.axis_index("core"), lax.axis_index("z")
    inverse = inverse_factor(whole_gram(gram_ref[...] + half_gram(other_ref)))
    width = TILES * TILE
    left_out[...] = left_ref[...]
    left = left_ref[...].T
    for q in range(4):
        block = z % 2 * 4 + q
        wide = jnp.where(core == z // 2, block_of(own_ref, block), block_of(other_ref, block))
        right = exact(inverse, wide) * math.sqrt(2 * LANES * width)
        at = slice(q * width, (q + 1) * width)
        right_ref[:, at] = right
        frozen_ref[:, at] = weight_ref[:, at].astype(F32) - exact(left, right) / math.sqrt(RANK)


def spread_kernel(terms_ref, copies_ref):
    lane = 4 * lax.axis_index("yl") + lax.axis_index("x")
    pairs = []
    for j in range(TILES):
        value = terms_ref[0, j].astype(F32)
        for i in range(1, GROUPS * LANES):
            value = value + terms_ref[i, j].astype(F32)
        pairs.append(split(value))
    for block in range(LANES):
        tile = (block - lane + LANES) % LANES
        low = pairs[0][1].astype(F32)
        for j in range(1, TILES):
            low = jnp.where(tile == j, pairs[j][1].astype(F32), low)
        for g in range(GROUPS):
            for j in range(TILES):
                copies_ref[g * LANES + block, j] = pairs[j][0]
            copies_ref[g * LANES + block, TILES] = low.astype(BF16)


def in_hbm(array):
    return pltpu.with_memory_space_constraint(array, pltpu.HBM)


def in_vmem(array):
    return pltpu.with_memory_space_constraint(array, pltpu.VMEM)


def total(send, applied, b, dtype=F32, low=False):
    keep = pl.pallas_call(
        keep_kernel, out_shape=jax.ShapeDtypeStruct(send.shape, F32), in_specs=[VMEM] * 2,
        out_specs=VMEM, compiler_params=PARAMS, name="keep",
    )(applied, in_vmem(b))
    got = lax.ppermute(send, "core", [(0, 1), (1, 0)])
    pair = (keep + got.astype(F32)).astype(BF16)
    terms = lax.all_to_all(pair, CHIPS, 0, 0, tiled=True)
    if low:
        copies = pl.pallas_call(
            spread_kernel,
            out_shape=jax.ShapeDtypeStruct((GROUPS * LANES, TILES + 1, 8, TILE), BF16),
            in_specs=[VMEM], out_specs=VMEM, compiler_params=PARAMS, name="spread",
        )(terms)
    else:
        mine = lax.optimization_barrier(jnp.sum(terms.astype(F32), axis=0)).astype(dtype)
        copies = jnp.broadcast_to(mine[None], terms.shape)
    own = lax.all_to_all(copies, CHIPS, 0, 0, tiled=True)
    return own, lax.ppermute(own, "core", [(0, 1), (1, 0)])


def local(acts, out_grads, test_matrix, weight):
    tokens, n = acts.shape
    rows, cols = weight.shape
    partial = (
        jax.ShapeDtypeStruct((GROUPS * LANES, TILES, 8, TILE), BF16),
        jax.ShapeDtypeStruct((RANK, tokens), BF16),
    )
    held = pltpu.VMEM((tokens, n), BF16)
    *made, acts, out_grads = pl.pallas_call(
        first_kernel, out_shape=(*partial, held, held), in_specs=[HBM] * 3,
        out_specs=(VMEM,) * 4,
        scratch_shapes=[
            pltpu.VMEM((RANK, n), BF16), pltpu.SemaphoreType.DMA((len(chunks(tokens, 256)),)),
            pltpu.SemaphoreType.DMA((8,)), pltpu.SemaphoreType.DMA(()),
        ],
        compiler_params=PARAMS, name="first",
    )(in_hbm(test_matrix.T), in_hbm(acts), in_hbm(out_grads))

    gram = jax.ShapeDtypeStruct((2 * RANK, 2 * RANK), F32)

    def step(wide, a, b):
        own, other = wide
        raw = jax.ShapeDtypeStruct((RANK, tokens), F32)
        terms = pltpu.VMEM((2 * RANK, n // 2), BF16)
        sums = pl.pallas_call(
            own_kernel, out_shape=(gram, raw), in_specs=[VMEM] * 2, out_specs=(VMEM,) * 2,
            scratch_shapes=[terms], compiler_params=PARAMS, name="own",
        )(own, in_vmem(a))
        return pl.pallas_call(
            next_kernel, out_shape=(*partial, jax.ShapeDtypeStruct((RANK, RANK), F32)),
            in_specs=[VMEM] * 5, out_specs=(VMEM,) * 3, scratch_shapes=[terms],
            compiler_params=PARAMS, name="step",
        )(other, *sums, in_vmem(a), in_vmem(b))

    sketch = total(*made, out_grads)
    *made, _ = step(sketch, out_grads, acts)
    cosketch = total(*made, acts, BF16)
    *made, _ = step(cosketch, acts, out_grads)
    power = total(*made, out_grads, low=True)
    *made, inverse = step(power, out_grads, acts)
    left = pl.pallas_call(
        left_kernel, out_shape=pltpu.VMEM((RANK, rows), F32), in_specs=[VMEM] * 3, out_specs=VMEM,
        compiler_params=PARAMS, name="left",
    )(*power, inverse)
    own, other = total(*made, acts)
    own_gram = pl.pallas_call(
        own_gram_kernel, out_shape=gram, in_specs=[VMEM], out_specs=VMEM, compiler_params=PARAMS,
        name="own_gram",
    )(own)
    frozen, left, right = pl.pallas_call(
        last_kernel,
        out_shape=(
            jax.ShapeDtypeStruct((rows, cols), F32), jax.ShapeDtypeStruct((RANK, rows), F32),
            jax.ShapeDtypeStruct((RANK, cols), F32),
        ),
        in_specs=[VMEM] * 5, out_specs=(VMEM,) * 3, compiler_params=PARAMS, name="last",
    )(own, other, own_gram, left, weight)
    return (frozen, left.T, right)


def solution(mesh):
    mesh = Mesh(mesh.devices.reshape(2, 2, 4, 2, 4), ("yh", "yl", "x", "core", "z"))
    row = ("yh", "yl", "x", "core")
    tokens = P((*row, "z"), None)
    return jax.shard_map(
        local, mesh=mesh, in_specs=(tokens, tokens, P(), P(row, "z")),
        out_specs=(P(row, "z"), P(row, None), P(None, "z")), check_vma=False,
    )
```

```python
import functools
import math

import jax
import jax.numpy as jnp
from jax import lax
from jax.experimental import pallas as pl
from jax.experimental.pallas import tpu as pltpu
from jax.sharding import Mesh, PartitionSpec as P

CHIPS = ("xl", "z", "y", "xh")
F32 = jnp.float32
BF16 = jnp.bfloat16
RANK = 64
VMEM = pl.BlockSpec(memory_space=pltpu.VMEM)
HBM = pl.BlockSpec(memory_space=pltpu.HBM)
PARAMS = pltpu.CompilerParams(vmem_limit_bytes=16 * 2**20)
GROUPS = 8
LANES = 8
TILES = 3
TILE = 128


def dot(left, right, contract):
    dims = (((contract[0],), (contract[1],)), ((), ()))
    return lax.dot_general(left, right, dims, preferred_element_type=F32)


def split(value):
    high = value.astype(BF16)
    return high, (value - high.astype(F32)).astype(BF16)


def exact(left, right):
    left_high, left_low = split(left)
    right_high, right_low = split(right)
    return dot(
        jnp.concatenate([left_high, left_high, left_low], 1),
        jnp.concatenate([right_high, right_low, right_high], 0),
        (1, 0),
    )


def inverse_factor(gram):
    shape = (RANK, RANK)
    eye = lax.broadcasted_iota(jnp.int32, shape, 0) == lax.broadcasted_iota(jnp.int32, shape, 1)
    both = jnp.concatenate([gram, eye.astype(F32)], 1)
    work = [both[8 * i : 8 * i + 8] for i in range(8)]
    tile = (8, 2 * RANK)
    sub = lax.broadcasted_iota(jnp.int32, tile, 0)
    done = []
    for p in range(8):
        cols = {
            i: [jnp.broadcast_to(work[i][:, k : k + 1], tile) for k in range(8 * p, 8 * p + 8)]
            for i in range(p, 8)
        }
        pivots = jnp.zeros(tile, F32)
        for j in range(8):
            pivot = jnp.broadcast_to(cols[p][j][j : j + 1], tile)
            inverse = 1.0 / pivot
            pivots = jnp.where(sub == j, pivot, pivots)
            row = jnp.broadcast_to(work[p][j : j + 1], tile)
            ahead = {q: jnp.broadcast_to(cols[p][q][j : j + 1], tile) for q in range(j + 1, 8)}
            for i in range(p, 8):
                scale = cols[i][j] * inverse
                if i == p:
                    scale = jnp.where(sub > j, scale, 0.0)
                work[i] = work[i] - scale * row
                for q in range(j + 1, 8):
                    cols[i][q] = cols[i][q] - scale * ahead[q]
        done.append(work[p] * lax.rsqrt(pivots))
    return jnp.concatenate(done, 0)[:, RANK:]


def lane_of(block, tile):
    return (block - 2 * tile + LANES) % LANES


def block_of(ref, block, low=False):
    def tile(g, j):
        at = g * LANES + lane_of(block, j)
        value = ref[at, j].astype(F32)
        return value + ref[at, TILES].astype(F32) if low else value

    rows = [jnp.concatenate([tile(g, j) for j in range(TILES)], 1) for g in range(GROUPS)]
    return jnp.concatenate(rows, 0)


def half_gram(ref, split_ref=None):
    width = TILES * TILE
    gram = jnp.zeros((2 * RANK, 2 * RANK), F32)
    for block in range(LANES):
        terms = jnp.concatenate(split(block_of(ref, block)), 0)
        if split_ref is not None:
            split_ref[:, block * width : (block + 1) * width] = terms
        gram = gram + dot(terms, terms, (1, 1))
    return gram


def whole_gram(gram):
    cross = gram[:RANK, RANK:] + gram[RANK:, :RANK]
    return gram[:RANK, :RANK] + (gram[RANK:, RANK:] + cross)


def columns(half, block):
    width = TILES * TILE
    return pl.ds(pl.multiple_of((2 * block + half) * width, width), width)


def blocks_of(ref, half, which):
    return jnp.concatenate([ref[:, columns(half, block)] for block in which], 1)


def half_product(terms, ref, half):
    raw = dot(terms, blocks_of(ref, half, range(LANES)), (1, 1))
    return raw[:RANK] + raw[RANK:]


def store_parts(part, index, ref):
    for h in range(2):
        for g in range(GROUPS):
            for j in range(TILES):
                start = (h * TILES + j) * TILE
                value = part[8 * g : 8 * g + 8, start : start + TILE]
                ref[g * LANES + lane_of(2 * index + h, j), j] = value.astype(ref.dtype)


def half_parts(applied, b_ref, half, ref):
    for i in range(LANES // 2):
        store_parts(dot(applied, blocks_of(b_ref, half, (2 * i, 2 * i + 1)), (1, 0)), i, ref)


def chunks(total, size):
    return [(s, min(size, total - s)) for s in range(0, total, size)]


def first_kernel(
    test_ref, a_ref, b_ref, send_ref, applied_ref, a_held, b_held, test_held, a_sems, b_sems, test_sem
):
    core = lax.axis_index("core")
    places = [columns(half, block) for half in (1 - core, core) for block in range(LANES)]
    rows = chunks(a_ref.shape[0], 256)
    test_copy = pltpu.make_async_copy(test_ref, test_held, test_sem)
    a_copies = [
        pltpu.make_async_copy(a_ref.at[pl.ds(s, n), :], a_held.at[pl.ds(s, n), :], a_sems.at[i])
        for i, (s, n) in enumerate(rows)
    ]
    b_copies = [
        pltpu.make_async_copy(b_ref.at[:, at], b_held.at[:, at], b_sems.at[i])
        for i, at in enumerate(places)
    ]
    for copy in [test_copy, *a_copies]:
        copy.start()
    test_copy.wait()
    test = test_held[...]
    applied = []
    for i, (copy, (s, n)) in enumerate(zip(a_copies, rows)):
        copy.wait()
        for later in b_copies[LANES * i : LANES * (i + 1)]:
            later.start()
        applied.append(dot(test, a_held[s : s + n, :], (1, 1)).astype(BF16))
    applied = jnp.concatenate(applied, 1)
    applied_ref[...] = applied
    for copy in b_copies[:LANES]:
        copy.wait()
    half_parts(applied, b_held, 1 - core, send_ref)
    for copy in b_copies[LANES:]:
        copy.wait()


def own_kernel(own_ref, a_ref, gram_ref, raw_ref, split_held):
    gram_ref[...] = half_gram(own_ref, split_held)
    raw_ref[...] = half_product(split_held[...], a_ref, lax.axis_index("core"))


def own_gram_kernel(own_ref, gram_ref):
    gram_ref[...] = half_gram(own_ref)


def next_kernel(
    other_ref, gram_ref, raw_ref, a_ref, b_ref, send_ref, applied_ref, inverse_ref, split_held
):
    other = 1 - lax.axis_index("core")
    inverse = inverse_factor(whole_gram(gram_ref[...] + half_gram(other_ref, split_held)))
    inverse_ref[...] = inverse
    raw = raw_ref[...] + half_product(split_held[...], a_ref, other)
    applied = exact(inverse, raw).astype(BF16)
    applied_ref[...] = applied
    half_parts(applied, b_ref, other, send_ref)


def keep_kernel(applied_ref, b_ref, keep_ref):
    half_parts(applied_ref[...], b_ref, lax.axis_index("core"), keep_ref)


def left_kernel(own_ref, other_ref, inverse_ref, left_ref):
    core = lax.axis_index("core")
    block = 2 * lax.axis_index("y") + lax.axis_index("xh")
    wide = jnp.where(
        core == lax.axis_index("xl"),
        block_of(own_ref, block, low=True),
        block_of(other_ref, block, low=True),
    )
    left = exact(inverse_ref[...], wide)
    rows = left_ref.shape[1]
    left = jnp.where(core == 0, left[:, :rows], left[:, rows:])
    left_ref[...] = left * math.sqrt(2 * LANES * TILES * TILE)


def last_kernel(
    own_ref, other_ref, gram_ref, left_ref, weight_ref, frozen_ref, left_out, right_ref
):
    core, z = lax.axis_index("core"), lax.axis_index("z")
    inverse = inverse_factor(whole_gram(gram_ref[...] + half_gram(other_ref)))
    width = TILES * TILE
    left_out[...] = left_ref[...]
    left = left_ref[...].T
    for q in range(4):
        block = 2 * z + q // 2
        wide = jnp.where(
            core == q % 2,
            block_of(own_ref, block, low=True),
            block_of(other_ref, block, low=True),
        )
        right = exact(inverse, wide) * math.sqrt(2 * LANES * width)
        at = slice(q * width, (q + 1) * width)
        right_ref[:, at] = right
        frozen_ref[:, at] = weight_ref[:, at].astype(F32) - exact(left, right) / math.sqrt(RANK)


def spread_kernel(terms_ref, copies_ref, *, rows):
    lane = 2 * lax.axis_index("y") + lax.axis_index("xh")
    pairs = []
    for j in range(TILES):
        value = terms_ref[0, j].astype(F32)
        for i in range(1, GROUPS * LANES):
            value = value + terms_ref[i, j].astype(F32)
        pairs.append(split(value))
    for block in range(LANES):
        for g in range(GROUPS):
            if rows:
                tile = (block - lane + LANES) % LANES
                step = 2
            else:
                tile = (g % 4 - lane // 2 + 4) % 4
                step = 1
            low = pairs[0][1].astype(F32)
            for j in range(1, TILES):
                low = jnp.where(tile == step * j, pairs[j][1].astype(F32), low)
                copies_ref[g * LANES + block, j] = pairs[j][0]
            copies_ref[g * LANES + block, 0] = pairs[0][0]
            copies_ref[g * LANES + block, TILES] = low.astype(BF16)


def in_hbm(array):
    return pltpu.with_memory_space_constraint(array, pltpu.HBM)


def in_vmem(array):
    return pltpu.with_memory_space_constraint(array, pltpu.VMEM)


def total(send, applied, b, dtype=F32, low=None):
    keep = pl.pallas_call(
        keep_kernel, out_shape=jax.ShapeDtypeStruct(send.shape, F32), in_specs=[VMEM] * 2,
        out_specs=VMEM, compiler_params=PARAMS, name="keep",
    )(applied, in_vmem(b))
    got = lax.ppermute(send, "core", [(0, 1), (1, 0)])
    pair = (keep + got.astype(F32)).astype(BF16)
    terms = lax.all_to_all(pair, CHIPS, 0, 0, tiled=True)
    if low:
        copies = pl.pallas_call(
            functools.partial(spread_kernel, rows=low == "rows"),
            out_shape=jax.ShapeDtypeStruct((GROUPS * LANES, TILES + 1, 8, TILE), BF16),
            in_specs=[VMEM], out_specs=VMEM, compiler_params=PARAMS, name="spread",
        )(terms)
    else:
        mine = lax.optimization_barrier(jnp.sum(terms.astype(F32), axis=0)).astype(dtype)
        copies = jnp.broadcast_to(mine[None], terms.shape)
    own = lax.all_to_all(copies, CHIPS, 0, 0, tiled=True)
    return own, lax.ppermute(own, "core", [(0, 1), (1, 0)])


def local(acts, out_grads, test_matrix, weight):
    tokens, n = acts.shape
    rows, cols = weight.shape
    partial = (
        jax.ShapeDtypeStruct((GROUPS * LANES, TILES, 8, TILE), BF16),
        jax.ShapeDtypeStruct((RANK, tokens), BF16),
    )
    held = pltpu.VMEM((tokens, n), BF16)
    *made, acts, out_grads = pl.pallas_call(
        first_kernel, out_shape=(*partial, held, held), in_specs=[HBM] * 3,
        out_specs=(VMEM,) * 4,
        scratch_shapes=[
            pltpu.VMEM((RANK, n), BF16), pltpu.SemaphoreType.DMA((len(chunks(tokens, 256)),)),
            pltpu.SemaphoreType.DMA((2 * LANES,)), pltpu.SemaphoreType.DMA(()),
        ],
        compiler_params=PARAMS, name="first",
    )(in_hbm(test_matrix.T), in_hbm(acts), in_hbm(out_grads))

    gram = jax.ShapeDtypeStruct((2 * RANK, 2 * RANK), F32)

    def step(wide, a, b):
        own, other = wide
        raw = jax.ShapeDtypeStruct((RANK, tokens), F32)
        terms = pltpu.VMEM((2 * RANK, n // 2), BF16)
        sums = pl.pallas_call(
            own_kernel, out_shape=(gram, raw), in_specs=[VMEM] * 2, out_specs=(VMEM,) * 2,
            scratch_shapes=[terms], compiler_params=PARAMS, name="own",
        )(own, in_vmem(a))
        return pl.pallas_call(
            next_kernel, out_shape=(*partial, jax.ShapeDtypeStruct((RANK, RANK), F32)),
            in_specs=[VMEM] * 5, out_specs=(VMEM,) * 3, scratch_shapes=[terms],
            compiler_params=PARAMS, name="step",
        )(other, *sums, in_vmem(a), in_vmem(b))

    sketch = total(*made, out_grads)
    *made, _ = step(sketch, out_grads, acts)
    cosketch = total(*made, acts, BF16)
    *made, _ = step(cosketch, acts, out_grads)
    power = total(*made, out_grads, low="rows")
    *made, inverse = step(power, out_grads, acts)
    left = pl.pallas_call(
        left_kernel, out_shape=pltpu.VMEM((RANK, rows), F32), in_specs=[VMEM] * 3, out_specs=VMEM,
        compiler_params=PARAMS, name="left",
    )(*power, inverse)
    own, other = total(*made, acts, low="columns")
    own_gram = pl.pallas_call(
        own_gram_kernel, out_shape=gram, in_specs=[VMEM], out_specs=VMEM, compiler_params=PARAMS,
        name="own_gram",
    )(own)
    frozen, left, right = pl.pallas_call(
        last_kernel,
        out_shape=(
            jax.ShapeDtypeStruct((rows, cols), F32), jax.ShapeDtypeStruct((RANK, rows), F32),
            jax.ShapeDtypeStruct((RANK, cols), F32),
        ),
        in_specs=[VMEM] * 5, out_specs=(VMEM,) * 3, compiler_params=PARAMS, name="last",
    )(own, other, own_gram, left, weight)
    return (frozen, left.T, right)


def solution(mesh):
    mesh = Mesh(mesh.devices.reshape(4, 2, 2, 2, 4), ("y", "xh", "xl", "core", "z"))
    row = ("y", "xh", "xl", "core")
    tokens = P((*row, "z"), None)
    return jax.shard_map(
        local, mesh=mesh, in_specs=(tokens, tokens, P(), P(row, "z")),
        out_specs=(P(row, "z"), P(row, None), P(None, "z")), check_vma=False,
    )
```

```python
import functools
import math

import jax
import jax.numpy as jnp
from jax import lax
from jax.experimental import pallas as pl
from jax.experimental.pallas import tpu as pltpu
from jax.sharding import Mesh, PartitionSpec as P

CHIPS = ("xl", "z", "y", "xh")
F32 = jnp.float32
BF16 = jnp.bfloat16
RANK = 64
VMEM = pl.BlockSpec(memory_space=pltpu.VMEM)
HBM = pl.BlockSpec(memory_space=pltpu.HBM)
PARAMS = pltpu.CompilerParams(vmem_limit_bytes=16 * 2**20)
GROUPS = 8
LANES = 8
TILES = 3
TILE = 128


def dot(left, right, contract):
    dims = (((contract[0],), (contract[1],)), ((), ()))
    return lax.dot_general(left, right, dims, preferred_element_type=F32)


def split(value):
    high = value.astype(BF16)
    return high, (value - high.astype(F32)).astype(BF16)


def exact(left, right):
    left_high, left_low = split(left)
    right_high, right_low = split(right)
    return dot(
        jnp.concatenate([left_high, left_high, left_low], 1),
        jnp.concatenate([right_high, right_low, right_high], 0),
        (1, 0),
    )


def inverse_factor(gram):
    shape = (RANK, RANK)
    eye = lax.broadcasted_iota(jnp.int32, shape, 0) == lax.broadcasted_iota(jnp.int32, shape, 1)
    both = jnp.concatenate([gram, eye.astype(F32)], 1)
    work = [both[8 * i : 8 * i + 8] for i in range(8)]
    tile = (8, 2 * RANK)
    sub = lax.broadcasted_iota(jnp.int32, tile, 0)
    done = []
    for p in range(8):
        cols = {
            i: [jnp.broadcast_to(work[i][:, k : k + 1], tile) for k in range(8 * p, 8 * p + 8)]
            for i in range(p, 8)
        }
        pivots = jnp.zeros(tile, F32)
        for j in range(8):
            pivot = jnp.broadcast_to(cols[p][j][j : j + 1], tile)
            inverse = 1.0 / pivot
            pivots = jnp.where(sub == j, pivot, pivots)
            row = jnp.broadcast_to(work[p][j : j + 1], tile)
            ahead = {q: jnp.broadcast_to(cols[p][q][j : j + 1], tile) for q in range(j + 1, 8)}
            for i in range(p, 8):
                scale = cols[i][j] * inverse
                if i == p:
                    scale = jnp.where(sub > j, scale, 0.0)
                work[i] = work[i] - scale * row
                for q in range(j + 1, 8):
                    cols[i][q] = cols[i][q] - scale * ahead[q]
        done.append(work[p] * lax.rsqrt(pivots))
    return jnp.concatenate(done, 0)[:, RANK:]


def lane_of(block, tile):
    return (block - 2 * tile + LANES) % LANES


def block_of(ref, block, low=False):
    def tile(g, j):
        at = g * LANES + lane_of(block, j)
        value = ref[at, j].astype(F32)
        return value + ref[at, TILES].astype(F32) if low else value

    rows = [jnp.concatenate([tile(g, j) for j in range(TILES)], 1) for g in range(GROUPS)]
    return jnp.concatenate(rows, 0)


def terms_of(dtype):
    return RANK if dtype == BF16 else 2 * RANK


def half_gram(ref, split_ref=None):
    width = TILES * TILE
    size = terms_of(ref.dtype)
    gram = jnp.zeros((size, size), F32)
    for block in range(LANES):
        terms = block_of(ref, block)
        terms = terms.astype(BF16) if size == RANK else jnp.concatenate(split(terms), 0)
        if split_ref is not None:
            split_ref[:, block * width : (block + 1) * width] = terms
        gram = gram + dot(terms, terms, (1, 1))
    return gram


def whole_gram(gram):
    if gram.shape[0] == RANK:
        return gram
    cross = gram[:RANK, RANK:] + gram[RANK:, :RANK]
    return gram[:RANK, :RANK] + (gram[RANK:, RANK:] + cross)


def columns(half, block):
    width = TILES * TILE
    return pl.ds(pl.multiple_of((2 * block + half) * width, width), width)


def blocks_of(ref, half, which):
    return jnp.concatenate([ref[:, columns(half, block)] for block in which], 1)


def half_product(terms, ref, half):
    raw = dot(terms, blocks_of(ref, half, range(LANES)), (1, 1))
    return raw if raw.shape[0] == RANK else raw[:RANK] + raw[RANK:]


def store_parts(part, index, ref):
    for h in range(2):
        for g in range(GROUPS):
            for j in range(TILES):
                start = (h * TILES + j) * TILE
                value = part[8 * g : 8 * g + 8, start : start + TILE]
                ref[g * LANES + lane_of(2 * index + h, j), j] = value.astype(ref.dtype)


def half_parts(applied, b_ref, half, ref):
    for i in range(LANES // 2):
        store_parts(dot(applied, blocks_of(b_ref, half, (2 * i, 2 * i + 1)), (1, 0)), i, ref)


def chunks(total, size):
    return [(s, min(size, total - s)) for s in range(0, total, size)]


def first_kernel(
    test_ref, a_ref, b_ref, send_ref, applied_ref, a_held, b_held, test_held, a_sems, b_sems, test_sem
):
    core = lax.axis_index("core")
    places = [columns(half, block) for half in (1 - core, core) for block in range(LANES)]
    rows = chunks(a_ref.shape[0], 256)
    test_copy = pltpu.make_async_copy(test_ref, test_held, test_sem)
    a_copies = [
        pltpu.make_async_copy(a_ref.at[pl.ds(s, n), :], a_held.at[pl.ds(s, n), :], a_sems.at[i])
        for i, (s, n) in enumerate(rows)
    ]
    b_copies = [
        pltpu.make_async_copy(b_ref.at[:, at], b_held.at[:, at], b_sems.at[i])
        for i, at in enumerate(places)
    ]
    for copy in [test_copy, *a_copies]:
        copy.start()
    test_copy.wait()
    test = test_held[...]
    applied = []
    for i, (copy, (s, n)) in enumerate(zip(a_copies, rows)):
        copy.wait()
        for later in b_copies[LANES * i : LANES * (i + 1)]:
            later.start()
        applied.append(dot(test, a_held[s : s + n, :], (1, 1)).astype(BF16))
    applied = jnp.concatenate(applied, 1)
    applied_ref[...] = applied
    for copy in b_copies[:LANES]:
        copy.wait()
    half_parts(applied, b_held, 1 - core, send_ref)
    for copy in b_copies[LANES:]:
        copy.wait()


def own_kernel(own_ref, a_ref, gram_ref, raw_ref, split_held):
    gram_ref[...] = half_gram(own_ref, split_held)
    raw_ref[...] = half_product(split_held[...], a_ref, lax.axis_index("core"))


def own_gram_kernel(own_ref, gram_ref):
    gram_ref[...] = half_gram(own_ref)


def next_kernel(
    other_ref, gram_ref, raw_ref, a_ref, b_ref, send_ref, applied_ref, inverse_ref, split_held
):
    other = 1 - lax.axis_index("core")
    inverse = inverse_factor(whole_gram(gram_ref[...] + half_gram(other_ref, split_held)))
    inverse_ref[...] = inverse
    raw = raw_ref[...] + half_product(split_held[...], a_ref, other)
    applied = exact(inverse, raw).astype(BF16)
    applied_ref[...] = applied
    half_parts(applied, b_ref, other, send_ref)


def keep_kernel(applied_ref, b_ref, keep_ref):
    half_parts(applied_ref[...], b_ref, lax.axis_index("core"), keep_ref)


def left_kernel(own_ref, other_ref, inverse_ref, left_ref):
    core = lax.axis_index("core")
    block = 2 * lax.axis_index("y") + lax.axis_index("xh")
    wide = jnp.where(
        core == lax.axis_index("xl"),
        block_of(own_ref, block, low=True),
        block_of(other_ref, block, low=True),
    )
    left = exact(inverse_ref[...], wide)
    rows = left_ref.shape[1]
    left = jnp.where(core == 0, left[:, :rows], left[:, rows:])
    left_ref[...] = left * math.sqrt(2 * LANES * TILES * TILE)


def last_kernel(
    own_ref, other_ref, gram_ref, left_ref, weight_ref, frozen_ref, left_out, right_ref
):
    core, z = lax.axis_index("core"), lax.axis_index("z")
    inverse = inverse_factor(whole_gram(gram_ref[...] + half_gram(other_ref)))
    width = TILES * TILE
    left_out[...] = left_ref[...]
    left = left_ref[...].T
    for q in range(4):
        block = 2 * z + q // 2
        wide = jnp.where(
            core == q % 2,
            block_of(own_ref, block, low=True),
            block_of(other_ref, block, low=True),
        )
        right = exact(inverse, wide) * math.sqrt(2 * LANES * width)
        at = slice(q * width, (q + 1) * width)
        right_ref[:, at] = right
        frozen_ref[:, at] = weight_ref[:, at].astype(F32) - exact(left, right) / math.sqrt(RANK)


def spread_kernel(terms_ref, copies_ref, *, rows):
    lane = 2 * lax.axis_index("y") + lax.axis_index("xh")
    pairs = []
    for j in range(TILES):
        value = terms_ref[0, j].astype(F32)
        for i in range(1, GROUPS * LANES):
            value = value + terms_ref[i, j].astype(F32)
        pairs.append(split(value))
    for block in range(LANES):
        for g in range(GROUPS):
            if rows:
                tile = (block - lane + LANES) % LANES
                step = 2
            else:
                tile = (g % 4 - lane // 2 + 4) % 4
                step = 1
            low = pairs[0][1].astype(F32)
            for j in range(1, TILES):
                low = jnp.where(tile == step * j, pairs[j][1].astype(F32), low)
                copies_ref[g * LANES + block, j] = pairs[j][0]
            copies_ref[g * LANES + block, 0] = pairs[0][0]
            copies_ref[g * LANES + block, TILES] = low.astype(BF16)


def in_hbm(array):
    return pltpu.with_memory_space_constraint(array, pltpu.HBM)


def in_vmem(array):
    return pltpu.with_memory_space_constraint(array, pltpu.VMEM)


def total(send, applied, b, dtype=F32, low=None):
    keep = pl.pallas_call(
        keep_kernel, out_shape=jax.ShapeDtypeStruct(send.shape, F32), in_specs=[VMEM] * 2,
        out_specs=VMEM, compiler_params=PARAMS, name="keep",
    )(applied, in_vmem(b))
    got = lax.ppermute(send, "core", [(0, 1), (1, 0)])
    pair = (keep + got.astype(F32)).astype(BF16)
    terms = lax.all_to_all(pair, CHIPS, 0, 0, tiled=True)
    if low:
        copies = pl.pallas_call(
            functools.partial(spread_kernel, rows=low == "rows"),
            out_shape=jax.ShapeDtypeStruct((GROUPS * LANES, TILES + 1, 8, TILE), BF16),
            in_specs=[VMEM], out_specs=VMEM, compiler_params=PARAMS, name="spread",
        )(terms)
    else:
        mine = lax.optimization_barrier(jnp.sum(terms.astype(F32), axis=0)).astype(dtype)
        copies = jnp.broadcast_to(mine[None], terms.shape)
    own = lax.all_to_all(copies, CHIPS, 0, 0, tiled=True)
    return own, lax.ppermute(own, "core", [(0, 1), (1, 0)])


def local(acts, out_grads, test_matrix, weight):
    tokens, n = acts.shape
    rows, cols = weight.shape
    partial = (
        jax.ShapeDtypeStruct((GROUPS * LANES, TILES, 8, TILE), BF16),
        jax.ShapeDtypeStruct((RANK, tokens), BF16),
    )
    held = pltpu.VMEM((tokens, n), BF16)
    *made, acts, out_grads = pl.pallas_call(
        first_kernel, out_shape=(*partial, held, held), in_specs=[HBM] * 3,
        out_specs=(VMEM,) * 4,
        scratch_shapes=[
            pltpu.VMEM((RANK, n), BF16), pltpu.SemaphoreType.DMA((len(chunks(tokens, 256)),)),
            pltpu.SemaphoreType.DMA((2 * LANES,)), pltpu.SemaphoreType.DMA(()),
        ],
        compiler_params=PARAMS, name="first",
    )(in_hbm(test_matrix.T), in_hbm(acts), in_hbm(out_grads))


    def gram_like(half):
        return jax.ShapeDtypeStruct((terms_of(half.dtype),) * 2, F32)

    def step(wide, a, b):
        own, other = wide
        raw = jax.ShapeDtypeStruct((RANK, tokens), F32)
        terms = pltpu.VMEM((terms_of(own.dtype), n // 2), BF16)
        sums = pl.pallas_call(
            own_kernel, out_shape=(gram_like(own), raw), in_specs=[VMEM] * 2, out_specs=(VMEM,) * 2,
            scratch_shapes=[terms], compiler_params=PARAMS, name="own",
        )(own, in_vmem(a))
        return pl.pallas_call(
            next_kernel, out_shape=(*partial, jax.ShapeDtypeStruct((RANK, RANK), F32)),
            in_specs=[VMEM] * 5, out_specs=(VMEM,) * 3, scratch_shapes=[terms],
            compiler_params=PARAMS, name="step",
        )(other, *sums, in_vmem(a), in_vmem(b))

    sketch = total(*made, out_grads)
    *made, _ = step(sketch, out_grads, acts)
    cosketch = total(*made, acts, BF16)
    *made, _ = step(cosketch, acts, out_grads)
    power = total(*made, out_grads, low="rows")
    *made, inverse = step(power, out_grads, acts)
    left = pl.pallas_call(
        left_kernel, out_shape=pltpu.VMEM((RANK, rows), F32), in_specs=[VMEM] * 3, out_specs=VMEM,
        compiler_params=PARAMS, name="left",
    )(*power, inverse)
    own, other = total(*made, acts, low="columns")
    own_gram = pl.pallas_call(
        own_gram_kernel, out_shape=gram_like(own), in_specs=[VMEM], out_specs=VMEM, compiler_params=PARAMS,
        name="own_gram",
    )(own)
    frozen, left, right = pl.pallas_call(
        last_kernel,
        out_shape=(
            jax.ShapeDtypeStruct((rows, cols), F32), jax.ShapeDtypeStruct((RANK, rows), F32),
            jax.ShapeDtypeStruct((RANK, cols), F32),
        ),
        in_specs=[VMEM] * 5, out_specs=(VMEM,) * 3, compiler_params=PARAMS, name="last",
    )(own, other, own_gram, left, weight)
    return (frozen, left.T, right)


def solution(mesh):
    mesh = Mesh(mesh.devices.reshape(4, 2, 2, 2, 4), ("y", "xh", "xl", "core", "z"))
    row = ("y", "xh", "xl", "core")
    tokens = P((*row, "z"), None)
    return jax.shard_map(
        local, mesh=mesh, in_specs=(tokens, tokens, P(), P(row, "z")),
        out_specs=(P(row, "z"), P(row, None), P(None, "z")), check_vma=False,
    )
```
